256 devices in a mesh: pipe: 8 (over y_hi, x), expert: 32 (over y_lo, z, core).
Axes of the slice: x: 4, y: 4 (y_hi: 2, y_lo: 2; y = y_hi * 2 + y_lo), z: 8, core: 2. Of those that a mesh axis runs over, the one named last changes fastest.
Arguments:
- fwd_in: bfloat16 [8, 4096, 3584], P('pipe', 'expert'), may hold values from -6 to 6
- fwd_route: int32 [8, 4096, 1], P('pipe', 'expert'), may hold values from 0 to 7; in each aligned block of 128 rows (0 to 127, 128 to 255, ..., all dimensions but the last counted through in order) at most 20 rows name the same one
- fwd_gate: float32 [8, 4096, 1], P('pipe', 'expert'), may hold values from 0.1 to 1
- bwd_saved: bfloat16 [8, 4096, 3584], P('pipe', 'expert'), may hold values from -6 to 6
- bwd_route: int32 [8, 4096, 1], P('pipe', 'expert'), may hold values from 0 to 7; in each aligned block of 128 rows (0 to 127, 128 to 255, ..., all dimensions but the last counted through in order) at most 20 rows name the same one
- bwd_gate: float32 [8, 4096, 1], P('pipe', 'expert'), may hold values from 0.1 to 1
- bwd_grad: bfloat16 [8, 4096, 3584], P('pipe', 'expert'), may hold values from -6 to 6
- w_in: bfloat16 [8, 32, 3584, 768], P('pipe', 'expert'), may hold values from -0.09375 to 0.09375
- w_out: bfloat16 [8, 32, 384, 3584], P('pipe', 'expert'), may hold values from -0.15625 to 0.15625
Outputs:
- fwd_out: bfloat16 [8, 4096, 3584], P('pipe', 'expert')
- bwd_out: bfloat16 [8, 4096, 3584], P('pipe', 'expert')
The draws below stay inside these ranges and needn't reach their ends.
Inputs may be any that keep to these rules, and one draw needn't show every extreme that they name: `fwd_route`: within the 128 rows of one device, no expert id is named by more than 20 rows. `bwd_route`: within the 128 rows of one device, no expert id is named by more than 20 rows.
All inputs are finite; a program needn't handle non-finite values.
Results may differ from the reference program's by a relative error of at most 0.0035.
Values may be sent and summed in bfloat16 or wider, within the bound.
A program may use at most 128 MiB of HBM per device.

```python
import math
import jax
import jax.numpy as jnp
import numpy as np
from jax import lax

D = 3584
FE = 1536
SPLIT = 4
TOP = 1
TOK_DEV = 128
HID = 384
EXPERTS = 8
CAP = 20
TOKENS = 4096
N_PIPE = 8
N_EXPERT = 32


def block_scale(key, extent, split, least, top_value):
    gain = 1.0
    for position, blocks in split:
        steps = jax.random.uniform(jax.random.fold_in(jax.random.fold_in(key, 6), position), (blocks,), jnp.float32, least / len(split), top_value / len(split))
        gain = gain * jnp.repeat(jnp.exp(steps), extent[position] // blocks).reshape((-1,) + (1,) * (len(extent) - 1 - position))
    return gain


def assign_block(key, own, number, rows, count, top, reach, lean):
    ranking = jax.random.permutation(key, count)
    packed, ordinary = portions_of(count, rows * top, reach, lean, True), portions_of(count, rows * top, reach, lean, False)
    places = jnp.arange(count)

    def named(sizes, rotation):
        used = int((sizes > 0).sum())
        fixed = max(1, used // 4)
        passed = fixed + (places - fixed + rotation * (used - fixed)) % max(1, count - fixed)
        return jnp.zeros((count,), jnp.int32).at[ranking[jnp.where(places < fixed, places, passed)]].set(jnp.asarray(sizes, jnp.int32))

    sizes = jnp.where(number % 4 == 0, named(packed, number // 4), named(ordinary, number - number // 4 - 1))
    mixed = jax.random.permutation(jax.random.fold_in(own, 3), count)
    giver, taker = mixed[0:count // 2 * 2:2], mixed[1:count // 2 * 2:2]
    margin = jnp.minimum(sizes[giver] - 1, reach - sizes[taker]) // 2
    margin = jnp.where((giver == ranking[0]) | (taker == ranking[0]) | (sizes[taker] == 0), 0, jnp.maximum(margin, 0))
    passed = jax.random.randint(jax.random.fold_in(own, 4), (count // 2,), 0, 1 << 20) % (margin + 1)
    sizes = sizes.at[giver].add(-passed).at[taker].add(passed)
    items = jnp.searchsorted(jnp.cumsum(sizes), jnp.arange(rows * top), side="right").astype(jnp.int32)
    grid = items.reshape(top, rows).T
    grid = grid[jax.random.permutation(jax.random.fold_in(own, 1), rows)]
    rotation = jax.random.randint(jax.random.fold_in(own, 2), (rows, 1), 0, top)
    return jnp.take_along_axis(grid, (jnp.arange(top)[None, :] + rotation) % top, axis=1)


def portions_of(amount, total, reach, lean, full):
    loads = [(1 << 20) // math.isqrt(grade ** lean) + 1 for grade in range(1, amount + 1)]
    largest = reach if full else min(reach, max(-(-total // amount), total * loads[0] // sum(loads)))
    least = 1 if total - largest >= amount - 1 else 0
    counts, surplus = [largest] + [least] * (amount - 1), total - largest - least * (amount - 1)
    while surplus > 0:
        movable = [i for i in range(1, amount) if counts[i] < largest] or [i for i in range(1, amount) if counts[i] < reach]
        pool, remaining = sum([loads[i] for i in movable]), surplus
        for i in movable:
            more = min(reach - counts[i], max(1, remaining * loads[i] // pool), surplus)
            counts[i] = counts[i] + more
            surplus = surplus - more
    return np.array(counts)


def noise(rng, shape, spread, limit, cuts=(), kind=jnp.bfloat16):
    level = block_scale(rng, shape, cuts, -0.22, 0.18) if cuts else 1.0
    array = jax.random.normal(rng, shape, jnp.float32) * spread * level
    return jnp.minimum(jnp.maximum(array, -limit), limit).astype(kind)


def setup_inputs(seed: int = 0) -> dict:
    key_of = jax.random.split(jax.random.key(seed), 10)
    fwd_in = noise(key_of[0], (N_PIPE, TOKENS, D), 1.0, 6.0, ((0, 8), (1, 32)))
    fwd_route_keys = jax.random.split(jax.random.fold_in(key_of[1], 1), N_PIPE * TOKENS // TOK_DEV)
    fwd_route_turns = jax.random.permutation(jax.random.fold_in(key_of[1], 3), N_PIPE * TOKENS // TOK_DEV)
    fwd_route = jax.vmap(lambda own, number: assign_block(jax.random.fold_in(key_of[1], 2), own, number, TOK_DEV, EXPERTS, TOP, CAP, 2))(fwd_route_keys, fwd_route_turns).reshape((N_PIPE, TOKENS, TOP))
    fwd_gate = jnp.clip(0.1 + 0.9 * jax.random.uniform(key_of[2], (N_PIPE, TOKENS, TOP), jnp.float32) ** block_scale(key_of[2], (N_PIPE, TOKENS, TOP), ((0, 8), (1, 32)), -0.2, 0.2), 0.1, 1.0)
    bwd_saved = noise(key_of[3], (N_PIPE, TOKENS, D), 1.0, 6.0, ((0, 8), (1, 32)))
    bwd_route_keys = jax.random.split(jax.random.fold_in(key_of[4], 1), N_PIPE * TOKENS // TOK_DEV)
    bwd_route_turns = jax.random.permutation(jax.random.fold_in(key_of[4], 3), N_PIPE * TOKENS // TOK_DEV)
    bwd_route = jax.vmap(lambda own, number: assign_block(jax.random.fold_in(key_of[4], 2), own, number, TOK_DEV, EXPERTS, TOP, CAP, 2))(bwd_route_keys, bwd_route_turns).reshape((N_PIPE, TOKENS, TOP))
    bwd_gate = jnp.clip(0.1 + 0.9 * jax.random.uniform(key_of[5], (N_PIPE, TOKENS, TOP), jnp.float32) ** block_scale(key_of[5], (N_PIPE, TOKENS, TOP), ((0, 8), (1, 32)), -0.2, 0.2), 0.1, 1.0)
    bwd_grad = noise(key_of[6], (N_PIPE, TOKENS, D), 1.0, 6.0, ((0, 8), (1, 32)))
    w_in = noise(key_of[7], (N_PIPE, N_EXPERT, D, 2 * HID), D ** -0.5, 0.09375, ((0, 8), (1, 32)))
    w_out = noise(key_of[8], (N_PIPE, N_EXPERT, HID, D), FE ** -0.5, 0.15625, ((0, 8), (1, 32)))
    return {"fwd_in": fwd_in, "fwd_route": fwd_route, "fwd_gate": fwd_gate, "bwd_saved": bwd_saved, "bwd_route": bwd_route, "bwd_gate": bwd_gate, "bwd_grad": bwd_grad, "w_in": w_in, "w_out": w_out}


def slice_forward(row_block, weight_in, weight_out):
    pre_act = jnp.dot(row_block, weight_in, preferred_element_type=jnp.float32)
    unit_count = weight_out.shape[0]
    gate_act = pre_act[:, :unit_count]
    up_act = pre_act[:, unit_count:]
    hidden = (gate_act * jax.nn.sigmoid(gate_act) * up_act).astype(jnp.bfloat16)
    return jnp.dot(hidden, weight_out, preferred_element_type=jnp.float32).astype(jnp.bfloat16)


def slice_backward(row_block, grad_block, weight_in, weight_out):
    pre_act = jnp.dot(row_block, weight_in, preferred_element_type=jnp.float32)
    unit_count = weight_out.shape[0]
    gate_act = pre_act[:, :unit_count]
    up_act = pre_act[:, unit_count:]
    sigmoid_gate = jax.nn.sigmoid(gate_act)
    hidden_grad = jnp.dot(grad_block, weight_out.T, preferred_element_type=jnp.float32)
    up_grad = hidden_grad * (gate_act * sigmoid_gate)
    gate_grad = hidden_grad * up_act * (sigmoid_gate * (1.0 + gate_act * (1.0 - sigmoid_gate)))
    pre_grad = jnp.concatenate([gate_grad, up_grad], axis=1).astype(jnp.bfloat16)
    return jnp.dot(pre_grad, weight_in.T, preferred_element_type=jnp.float32).astype(jnp.bfloat16)


def slot_positions(routing):
    tok_count = routing.shape[0]
    onehot = (routing[:, :, None] == jnp.arange(EXPERTS, dtype=jnp.int32)[None, None, :]).astype(jnp.int32)
    flat_hits = onehot.reshape(tok_count * TOP, EXPERTS)
    earlier = (jnp.cumsum(flat_hits, axis=0) - flat_hits).astype(jnp.int32)
    return jnp.sum(earlier * flat_hits, axis=1).astype(jnp.int32).reshape(tok_count, TOP)


def run_layer(tokens, routing, gate_prob, weight_in, weight_out, grads):
    tok_count = tokens.shape[0]
    slot_index = slot_positions(routing)
    room = N_EXPERT * CAP
    spread_rows = jnp.broadcast_to(tokens[:, None, :], (tok_count, TOP, D))
    buffer = jnp.zeros((EXPERTS, room, D), jnp.bfloat16).at[routing, slot_index].set(spread_rows)
    weights_in = weight_in.reshape(EXPERTS, SPLIT, D, 2 * HID)
    weights_out = weight_out.reshape(EXPERTS, SPLIT, HID, D)
    if grads is None:
        def per_expert(items):
            rows_here, w_one, w_two = items
            summed = jnp.zeros((room, D), jnp.float32)
            for piece in range(SPLIT):
                summed = summed + slice_forward(rows_here, w_one[piece], w_two[piece]).astype(jnp.float32)
            return summed
        results = lax.map(per_expert, (buffer, weights_in, weights_out))
        base = tokens
    else:
        grad_rows = jnp.broadcast_to(grads[:, None, :], (tok_count, TOP, D))
        grad_buffer = jnp.zeros((EXPERTS, room, D), jnp.bfloat16).at[routing, slot_index].set(grad_rows)

        def per_expert(items):
            rows_here, grads_here, w_one, w_two = items
            summed = jnp.zeros((room, D), jnp.float32)
            for piece in range(SPLIT):
                summed = summed + slice_backward(rows_here, grads_here, w_one[piece], w_two[piece]).astype(jnp.float32)
            return summed
        results = lax.map(per_expert, (buffer, grad_buffer, weights_in, weights_out))
        base = grads
    picked = results[routing, slot_index]
    mixture = jnp.sum(gate_prob[:, :, None] * picked, axis=1)
    return (base.astype(jnp.float32) + mixture).astype(jnp.bfloat16)


def reference(fwd_in, fwd_route, fwd_gate, bwd_saved, bwd_route, bwd_gate, bwd_grad, w_in, w_out):
    arrived = jnp.roll(fwd_in, 1, axis=0)
    returned = jnp.roll(bwd_grad, -1, axis=0)
    forward_list = []
    backward_list = []
    for rank in range(N_PIPE):
        forward_list.append(run_layer(arrived[rank], fwd_route[rank], fwd_gate[rank], w_in[rank], w_out[rank], None))
        backward_list.append(run_layer(bwd_saved[rank], bwd_route[rank], bwd_gate[rank], w_in[rank], w_out[rank], returned[rank]))
    return jnp.stack(forward_list), jnp.stack(backward_list)
```

```python
import jax
import jax.numpy as jnp
from jax import lax
from jax.experimental import pallas as pl
from jax.experimental.pallas import tpu as pltpu
from jax.sharding import PartitionSpec as P

MESH = pl.DeviceIdType.MESH
TOK = 128
D = 3584
HID = 384
ROWS = 16
CHUNK = 896
CHUNKS = 4
FOLD = 4
UNITS = 8
ENTRY = UNITS * ROWS
ALL_ROWS = 4 * ENTRY
LEFT = 128
OFFSETS = (0, -1, 2, -3)
ORDER = (4, 0, 1, 2, 3)
SAVED, ARRIVED, RETURNED = 0, 1, 2
FORWARD, BACKWARD = 0, 1
F32 = jnp.float32
BF16 = jnp.bfloat16


def dot(a, b):
    return lax.dot_general(a, b, (((1,), (0,)), ((), ())), preferred_element_type=F32)


def dot_t(a, b):
    return lax.dot_general(a, b, (((1,), (1,)), ((), ())), preferred_element_type=F32)


def iota(shape, dim):
    return lax.broadcasted_iota(jnp.int32, shape, dim)


def one_hot(mask):
    return jnp.where(mask, 1.0, 0.0).astype(BF16)


def kernel(
    fwd_in, fwd_route, fwd_gate, bwd_saved, bwd_route, bwd_gate, bwd_grad, w_in, w_out,
    fwd_out, bwd_out,
    saved, arrived, returned, win, wout, packed, land, pre_f, pre_b, hidden, pre_grad,
    own, cross, sib, pair_out, pair_in, total, back, result,
    send_a, recv_a, send_b, recv_b, send_c, recv_c, send_d, recv_d,
    send_s, recv_s, send_p, recv_p, send_r, recv_r, send_m, recv_m, load, store,
):
    pipe = lax.axis_index("pipe")
    place = lax.axis_index("expert")
    y = lax.div(place, 16)
    z = lax.rem(lax.div(place, 2), 8)
    core = lax.rem(place, 2)
    side = 1 - 2 * lax.rem(z, 2)

    def device(pipe_at, y_at, z_at, core_at):
        return (pipe_at, y_at * 16 + z_at * 2 + core_at)

    def at(y_step, z_step):
        return lax.rem(y + y_step, 2), lax.rem(z + z_step + 8, 8)

    targets, experts, sources = [], [], []
    for i in range(4):
        for y_step in range(2):
            y_to, z_to = at(y_step, OFFSETS[i] * side)
            targets.append(device(pipe, y_to, z_to, core))
            experts.append(y_to * 4 + lax.div(z_to, 2))
            y_from, z_from = at(y_step, -i * side)
            sources.append(device(pipe, y_from, z_from, core))
    sibling = device(pipe, y, z, 1 - core)
    partner = device(pipe, y, lax.rem(z + side + 8, 8), core)
    after = (lax.rem(pipe + 1, 8), place)
    before = (lax.rem(pipe + 7, 8), place)

    loads = [pltpu.make_async_copy(bwd_saved, saved, load.at[0])]
    for k in range(CHUNKS):
        columns = pl.ds(k * CHUNK, CHUNK)
        loads.append(pltpu.make_async_copy(w_in.at[columns], win.at[k], load.at[1 + k]))
        loads.append(pltpu.make_async_copy(w_out.at[:, columns], wout.at[k], load.at[5 + k]))
    for copy in loads:
        copy.start()

    barrier = pltpu.get_barrier_semaphore()
    peers = targets[1:] + sources[4:6] + [sibling, partner, after, before]
    for peer in peers:
        pl.semaphore_signal(barrier, inc=1, device_id=peer, device_id_type=MESH)
    pl.semaphore_wait(barrier, len(peers))

    def remote(src, dst, send, recv, to):
        return pltpu.make_async_remote_copy(
            src_ref=src, dst_ref=dst, send_sem=send, recv_sem=recv, device_id=to, device_id_type=MESH
        )

    moves = [
        remote(fwd_in, arrived, send_m.at[0], recv_m.at[0], after),
        remote(bwd_grad, returned, send_m.at[1], recv_m.at[1], before),
    ]
    for copy in moves:
        copy.start()

    def unit_experts(shape, dim):
        unit = lax.div(iota(shape, dim), ROWS)
        named = jnp.zeros(shape, jnp.int32)
        for u in range(UNITS):
            named = jnp.where(unit == u, experts[u], named)
        return named

    def pack(flow, values, route):
        square = (TOK, TOK)
        by_row = jnp.broadcast_to(route[...], square).astype(F32)
        by_lane = by_row.T
        earlier = iota(square, 0) < iota(square, 1)
        slot = jnp.sum(jnp.where((by_row == by_lane) & earlier, 1.0, 0.0), axis=0, keepdims=True)
        named = unit_experts(square, 0).astype(F32) == by_lane
        row = lax.rem(iota(square, 0), ROWS)
        main = one_hot(named & (row.astype(F32) == slot))
        late = named & ((ROWS + lax.rem(row, 4)).astype(F32) == slot)

        def put(k, rows):
            packed[flow, k] = rows.astype(BF16)
            land[flow, k, 0:ROWS] = packed[flow, k, 0:ROWS]
            for u in range(1, UNITS):
                block = pl.ds(u * ROWS, ROWS)
                remote(
                    packed.at[flow, k, block], land.at[flow, k, block],
                    send_a.at[flow, k], recv_a.at[flow, k], targets[u],
                ).start()

        for k in range(CHUNKS):
            put(k, dot(main, values[:, k * CHUNK : (k + 1) * CHUNK]))
        rows = jnp.zeros((ENTRY, CHUNK), F32)
        for k in range(CHUNKS):
            mine = one_hot(late & (lax.div(row, 4) == k))
            rows = rows + dot(mine, values[:, k * CHUNK : (k + 1) * CHUNK])
        put(FOLD, rows)

    def direct(flow, k):
        block = pl.ds(ROWS, ENTRY - ROWS)
        return remote(
            packed.at[flow, k, block], land.at[flow, k, block],
            send_a.at[flow, k], recv_a.at[flow, k], targets[1],
        )

    def group(flow, k, index):
        return land.at[flow, k, pl.ds(index * ENTRY, ENTRY)]

    def to_partner(flow, k):
        return remote(
            group(flow, k, 0), group(flow, k, 1), send_b.at[flow, k], recv_b.at[flow, k], partner
        )

    def to_sibling(flow, k):
        return remote(
            group(flow, k, 0), group(flow, k, 2), send_c.at[flow, k], recv_c.at[flow, k], sibling
        )

    def on_to_sibling(flow, k):
        return remote(
            group(flow, k, 1), group(flow, k, 3), send_d.at[flow, k], recv_d.at[flow, k], sibling
        )

    def enter(flow, k):
        direct(flow, k).wait_recv()
        to_partner(flow, k).start()
        to_sibling(flow, k).start()

    def pass_on(flow, k):
        to_partner(flow, k).wait_recv()
        on_to_sibling(flow, k).start()

    def ready(flow):
        for k in range(CHUNKS + 1):
            to_sibling(flow, k).wait_recv()
            on_to_sibling(flow, k).wait_recv()

    def unfold(flow, k):
        shape = (LEFT, ALL_ROWS)
        row = iota(shape, 0)
        taken = lax.div(row, 4) * ROWS + k * 4 + lax.rem(row, 4)
        return dot(one_hot(iota(shape, 1) == taken), land[flow, FOLD]).astype(BF16)

    def fold(k, rows):
        shape = (ALL_ROWS, LEFT)
        column = iota(shape, 1)
        taken = lax.div(column, 4) * ROWS + k * 4 + lax.rem(column, 4)
        return dot(one_hot(iota(shape, 0) == taken), rows)

    def activate_in(flow, out):
        out[...] = jnp.zeros_like(out)

        @pl.loop(0, CHUNKS)
        def _(k):
            weight = win[k]
            out[0:ALL_ROWS] += dot(land[flow, k], weight)
            out[ALL_ROWS:] += dot(unfold(flow, k), weight)

    def make_hidden():
        @pl.loop(0, (ALL_ROWS + LEFT) // LEFT)
        def _(n):
            rows = pl.ds(pl.multiple_of(n * LEFT, LEFT), LEFT)
            gate_act = pre_f[rows, :HID]
            hidden[rows] = (gate_act * jax.nn.sigmoid(gate_act) * pre_f[rows, HID:]).astype(BF16)

    def make_pre_grad():
        pre_f[...] = jnp.zeros_like(pre_f)

        @pl.loop(0, CHUNKS)
        def _(k):
            weight = wout[k]
            pre_f[0:ALL_ROWS, :HID] += dot_t(land[RETURNED, k], weight)
            pre_f[ALL_ROWS:, :HID] += dot_t(unfold(RETURNED, k), weight)

        @pl.loop(0, (ALL_ROWS + LEFT) // LEFT)
        def _(n):
            rows = pl.ds(pl.multiple_of(n * LEFT, LEFT), LEFT)
            hidden_grad = pre_f[rows, :HID]
            gate_act = pre_b[rows, :HID]
            up_act = pre_b[rows, HID:]
            sigmoid_gate = jax.nn.sigmoid(gate_act)
            up_grad = hidden_grad * (gate_act * sigmoid_gate)
            slope = sigmoid_gate * (1.0 + gate_act * (1.0 - sigmoid_gate))
            pre_grad[rows, :HID] = (hidden_grad * up_act * slope).astype(BF16)
            pre_grad[rows, HID:] = up_grad.astype(BF16)

    def product(way, rows, k):
        if way == FORWARD:
            return dot(hidden[rows], wout[k])
        return dot_t(pre_grad[rows], win[k])

    def swap(way, k):
        return remote(cross.at[k], sib.at[way, k], send_s.at[way, k], recv_s.at[way, k], sibling)

    def to_exit(way, k):
        return remote(pair_out.at[k], pair_in.at[way, k], send_p.at[way, k], recv_p.at[way, k], partner)

    def homeward(way, k):
        block = pl.ds(ROWS, ENTRY - ROWS)
        return remote(
            total.at[k, block], back.at[way, k, block], send_r.at[way, k], recv_r.at[way, k], sources[1]
        )

    def work(way, k):
        if way == BACKWARD:
            swap(FORWARD, k).wait_send()
        if k < CHUNKS:
            rows = product(way, slice(0, ALL_ROWS), k).astype(BF16)
            own[k] = rows[: 2 * ENTRY]
            cross[k] = rows[2 * ENTRY :]
        else:
            rows = jnp.zeros((ALL_ROWS, CHUNK), F32)
            for c in range(CHUNKS):
                rows = rows + fold(c, product(way, slice(ALL_ROWS, ALL_ROWS + LEFT), c).astype(BF16))
            rows = rows.astype(BF16)
            own[k] = rows[: 2 * ENTRY]
            cross[k] = rows[2 * ENTRY :]
        swap(way, k).start()

    def add_sibling(way, k):
        swap(way, k).wait_recv()
        if way == BACKWARD:
            to_exit(FORWARD, k).wait_send()
        rows = own[k, ENTRY:].astype(F32) + sib[way, k, ENTRY:].astype(F32)
        pair_out[k] = rows.astype(BF16)
        to_exit(way, k).start()

    def leave(way, k):
        to_exit(way, k).wait_recv()
        if way == BACKWARD:
            homeward(FORWARD, k).wait_send()
        rows = own[k, :ENTRY].astype(F32) + sib[way, k, :ENTRY].astype(F32)
        total[k] = (rows + pair_in[way, k].astype(F32)).astype(BF16)
        back[way, k, 0:ROWS] = total[k, 0:ROWS]
        for u in range(1, UNITS):
            block = pl.ds(u * ROWS, ROWS)
            remote(
                total.at[k, block], back.at[way, k, block],
                send_r.at[way, k], recv_r.at[way, k], sources[u],
            ).start()

    def written(way, k):
        columns = pl.ds(k * CHUNK, CHUNK)
        out = fwd_out if way == FORWARD else bwd_out
        return pltpu.make_async_copy(result.at[way, :, columns], out.at[:, columns], store.at[way, k])

    def finish(way, k):
        homeward(way, k).wait_recv()
        if k == FOLD:
            return
        route, gate, base = (
            (fwd_route, fwd_gate, arrived) if way == FORWARD else (bwd_route, bwd_gate, returned)
        )
        square = (TOK, TOK)
        by_row = jnp.broadcast_to(route[...], square).astype(F32)
        by_lane = by_row.T
        earlier = iota(square, 1) < iota(square, 0)
        slot = jnp.sum(jnp.where((by_row == by_lane) & earlier, 1.0, 0.0), axis=1, keepdims=True)
        named = unit_experts(square, 1).astype(F32) == by_row
        column = lax.rem(iota(square, 1), ROWS)
        main = one_hot(named & (column.astype(F32) == slot))
        late = named & ((ROWS + lax.rem(column, 4)).astype(F32) == slot)
        mine = one_hot(late & (lax.div(column, 4) == k))
        mixture = dot(main, back[way, k]) + dot(mine, back[way, FOLD])
        at_columns = slice(k * CHUNK, (k + 1) * CHUNK)
        result[way, :, at_columns] = (
            base[:, at_columns].astype(F32) + gate[...] * mixture
        ).astype(BF16)
        written(way, k).start()

    loads[0].wait()
    pack(SAVED, saved, bwd_route)
    for k in range(CHUNKS + 1):
        enter(SAVED, k)
        if k:
            pass_on(SAVED, k - 1)
        if k == 3:
            moves[0].wait_recv()
            pack(ARRIVED, arrived, fwd_route)
    pass_on(SAVED, FOLD)
    for k in range(CHUNKS + 1):
        enter(ARRIVED, k)
        if k:
            pass_on(ARRIVED, k - 1)
        else:
            for copy in loads[1:]:
                copy.wait()
            ready(SAVED)
            activate_in(SAVED, pre_b)
        if k == 3:
            moves[1].wait_recv()
            pack(RETURNED, returned, bwd_route)
    pass_on(ARRIVED, FOLD)
    for k in range(CHUNKS + 1):
        enter(RETURNED, k)
        if k:
            pass_on(RETURNED, k - 1)
        else:
            ready(ARRIVED)
            activate_in(ARRIVED, pre_f)
            make_hidden()
        work(FORWARD, ORDER[k])
    pass_on(RETURNED, FOLD)
    for k in ORDER:
        add_sibling(FORWARD, k)
    ready(RETURNED)
    make_pre_grad()
    for j, k in enumerate(ORDER):
        leave(FORWARD, k)
        work(BACKWARD, k)
        if j:
            add_sibling(BACKWARD, ORDER[j - 1])
    add_sibling(BACKWARD, ORDER[-1])
    for k in ORDER:
        leave(BACKWARD, k)
        finish(FORWARD, k)
    for k in ORDER:
        finish(BACKWARD, k)

    for copy in moves:
        copy.wait_send()
    for flow in range(3):
        for k in range(CHUNKS + 1):
            direct(flow, k).wait_send()
            to_partner(flow, k).wait_send()
            to_sibling(flow, k).wait_send()
            on_to_sibling(flow, k).wait_send()
    for k in range(CHUNKS + 1):
        swap(BACKWARD, k).wait_send()
        to_exit(BACKWARD, k).wait_send()
        homeward(BACKWARD, k).wait_send()
    for way in (FORWARD, BACKWARD):
        for k in range(CHUNKS):
            written(way, k).wait()


def local(fwd_in, fwd_route, fwd_gate, bwd_saved, bwd_route, bwd_gate, bwd_grad, w_in, w_out):
    any_place = pl.BlockSpec(memory_space=pl.ANY)
    vmem = pl.BlockSpec(memory_space=pltpu.VMEM)
    tokens = (TOK, D)
    parts = CHUNKS + 1
    dma = pltpu.SemaphoreType.DMA
    fwd_out, bwd_out = pl.pallas_call(
        kernel,
        out_shape=[jax.ShapeDtypeStruct(tokens, BF16)] * 2,
        in_specs=[any_place, vmem, vmem, any_place, vmem, vmem, any_place, any_place, any_place],
        out_specs=[any_place, any_place],
        scratch_shapes=[
            pltpu.VMEM(tokens, BF16),
            pltpu.VMEM(tokens, BF16),
            pltpu.VMEM(tokens, BF16),
            pltpu.VMEM((CHUNKS, CHUNK, 2 * HID), BF16),
            pltpu.VMEM((CHUNKS, HID, CHUNK), BF16),
            pltpu.VMEM((3, parts, ENTRY, CHUNK), BF16),
            pltpu.VMEM((3, parts, ALL_ROWS, CHUNK), BF16),
            pltpu.VMEM((ALL_ROWS + LEFT, 2 * HID), F32),
            pltpu.VMEM((ALL_ROWS + LEFT, 2 * HID), F32),
            pltpu.VMEM((ALL_ROWS + LEFT, HID), BF16),
            pltpu.VMEM((ALL_ROWS + LEFT, 2 * HID), BF16),
            pltpu.VMEM((parts, 2 * ENTRY, CHUNK), BF16),
            pltpu.VMEM((parts, 2 * ENTRY, CHUNK), BF16),
            pltpu.VMEM((2, parts, 2 * ENTRY, CHUNK), BF16),
            pltpu.VMEM((parts, ENTRY, CHUNK), BF16),
            pltpu.VMEM((2, parts, ENTRY, CHUNK), BF16),
            pltpu.VMEM((parts, ENTRY, CHUNK), BF16),
            pltpu.VMEM((2, parts, ENTRY, CHUNK), BF16),
            pltpu.VMEM((2, TOK, D), BF16),
        ]
        + [dma((3, parts))] * 8
        + [dma((2, parts))] * 6
        + [dma((2,))] * 2
        + [dma((9,)), dma((2, CHUNKS))],
        compiler_params=pltpu.CompilerParams(
            collective_id=0, has_side_effects=True, vmem_limit_bytes=60 * 2**20
        ),
        cost_estimate=pl.CostEstimate(
            flops=14 * 10**9, bytes_accessed=14 * 10**6, transcendentals=500_000
        ),
    )(
        fwd_in[0], fwd_route[0], fwd_gate[0], bwd_saved[0], bwd_route[0], bwd_gate[0], bwd_grad[0],
        w_in[0, 0], w_out[0, 0],
    )
    return fwd_out[None], bwd_out[None]


def solution(mesh):
    rows = P("pipe", "expert", None)
    pieces = P("pipe", "expert", None, None)
    return jax.shard_map(
        local,
        mesh=mesh,
        in_specs=(rows,) * 7 + (pieces,) * 2,
        out_specs=(rows, rows),
        check_vma=False,
    )
```

```python
import jax
import jax.numpy as jnp
from jax import lax
from jax.experimental import pallas as pl
from jax.experimental.pallas import tpu as pltpu
from jax.sharding import PartitionSpec as P

MESH = pl.DeviceIdType.MESH
TOK = 128
D = 3584
HID = 384
ROWS = 16
CHUNK = 896
CHUNKS = 4
FOLD = 4
UNITS = 8
ENTRY = UNITS * ROWS
ALL_ROWS = 4 * ENTRY
LEFT = 128
OFFSETS = (0, -1, 2, -3)
ORDER = (0, 4, 1, 2, 3)
MOVE_AT = (0, 4)
LAG = 4
AHEAD = 5
SAVED, ARRIVED, RETURNED = 0, 1, 2
FORWARD, BACKWARD = 0, 1
F32 = jnp.float32
BF16 = jnp.bfloat16


def dot(a, b):
    return lax.dot_general(a, b, (((1,), (0,)), ((), ())), preferred_element_type=F32)


def dot_t(a, b):
    return lax.dot_general(a, b, (((1,), (1,)), ((), ())), preferred_element_type=F32)


def iota(shape, dim):
    return lax.broadcasted_iota(jnp.int32, shape, dim)


def one_hot(mask):
    return jnp.where(mask, 1.0, 0.0).astype(BF16)


def kernel(
    fwd_in, fwd_route, fwd_gate, bwd_saved, bwd_route, bwd_gate, bwd_grad, w_in, w_out,
    fwd_out, bwd_out,
    saved, arrived, returned, win, wout, packing, placing, packed, land, pre_f, pre_b, hidden, pre_grad,
    own, cross, sib, pair_out, pair_in, total, back, result,
    send_a, recv_a, send_b, recv_b, send_c, recv_c, send_d, recv_d,
    send_s, recv_s, send_p, recv_p, send_r, recv_r, send_m, recv_m, load, store,
):
    pipe = lax.axis_index("pipe")
    place = lax.axis_index("expert")
    y = lax.div(place, 16)
    z = lax.rem(lax.div(place, 2), 8)
    core = lax.rem(place, 2)
    side = 1 - 2 * lax.rem(z, 2)

    def device(pipe_at, y_at, z_at, core_at):
        return (pipe_at, y_at * 16 + z_at * 2 + core_at)

    def at(y_step, z_step):
        return lax.rem(y + y_step, 2), lax.rem(z + z_step + 8, 8)

    targets, experts, sources = [], [], []
    for i in range(4):
        for y_step in range(2):
            y_to, z_to = at(y_step, OFFSETS[i] * side)
            targets.append(device(pipe, y_to, z_to, core))
            experts.append(y_to * 4 + lax.div(z_to, 2))
            y_from, z_from = at(y_step, -i * side)
            sources.append(device(pipe, y_from, z_from, core))
    sibling = device(pipe, y, z, 1 - core)
    partner = device(pipe, y, lax.rem(z + side + 8, 8), core)
    after = (lax.rem(pipe + 1, 8), place)
    before = (lax.rem(pipe + 7, 8), place)

    loads = [pltpu.make_async_copy(bwd_saved, saved, load.at[0])]
    for k in range(CHUNKS):
        columns = pl.ds(k * CHUNK, CHUNK)
        loads.append(pltpu.make_async_copy(w_in.at[columns], win.at[k], load.at[1 + k]))
        loads.append(pltpu.make_async_copy(w_out.at[:, columns], wout.at[k], load.at[5 + k]))
    for copy in loads:
        copy.start()

    barrier = pltpu.get_barrier_semaphore()
    peers = targets[1:] + sources[4:6] + [sibling, partner, after, before]
    for peer in peers:
        pl.semaphore_signal(barrier, inc=1, device_id=peer, device_id_type=MESH)

    def remote(src, dst, send, recv, to):
        return pltpu.make_async_remote_copy(
            src_ref=src, dst_ref=dst, send_sem=send, recv_sem=recv, device_id=to, device_id_type=MESH
        )

    def move(way, k):
        columns = pl.ds(k * CHUNK, CHUNK)
        src, dst, to = ((fwd_in, arrived, after), (bwd_grad, returned, before))[way]
        return remote(src.at[:, columns], dst.at[:, columns], send_m.at[way, k], recv_m.at[way, k], to)

    def unit_experts(shape, dim):
        unit = lax.div(iota(shape, dim), ROWS)
        named = jnp.zeros(shape, jnp.int32)
        for u in range(UNITS):
            named = jnp.where(unit == u, experts[u], named)
        return named

    def make_masks(way):
        square = (TOK, TOK)
        route = (fwd_route, bwd_route)[way]
        by_lane = jnp.broadcast_to(route[...], square).astype(F32)
        by_row = by_lane.T
        same = by_row == by_lane
        lane, sublane = iota(square, 1), iota(square, 0)

        slot = jnp.sum(jnp.where(same & (sublane < lane), 1.0, 0.0), axis=0, keepdims=True)
        named = unit_experts(square, 0).astype(F32) == by_lane
        row = lax.rem(sublane, ROWS)
        packing[way, FOLD] = one_hot(named & (row.astype(F32) == slot))
        late = named & ((ROWS + lax.rem(row, 4)).astype(F32) == slot)
        for k in range(CHUNKS):
            packing[way, k] = one_hot(late & (lax.div(row, 4) == k))

        slot = jnp.sum(jnp.where(same & (lane < sublane), 1.0, 0.0), axis=1, keepdims=True)
        named = unit_experts(square, 1).astype(F32) == by_row
        column = lax.rem(lane, ROWS)
        placing[way, FOLD] = one_hot(named & (column.astype(F32) == slot))
        late = named & ((ROWS + lax.rem(column, 4)).astype(F32) == slot)
        for k in range(CHUNKS):
            placing[way, k] = one_hot(late & (lax.div(column, 4) == k))

    def pack(flow, k):
        values = (saved, arrived, returned)[flow]
        way = FORWARD if flow == ARRIVED else BACKWARD
        if k < CHUNKS:
            rows = dot(packing[way, FOLD], values[:, k * CHUNK : (k + 1) * CHUNK])
        else:
            rows = jnp.zeros((ENTRY, CHUNK), F32)
            for c in range(CHUNKS):
                rows = rows + dot(packing[way, c], values[:, c * CHUNK : (c + 1) * CHUNK])
        packed[flow, k] = rows.astype(BF16)
        land[flow, k, 0:ROWS] = packed[flow, k, 0:ROWS]

    def send(flow, k):
        for u in range(1, UNITS):
            block = pl.ds(u * ROWS, ROWS)
            remote(
                packed.at[flow, k, block], land.at[flow, k, block],
                send_a.at[flow, k], recv_a.at[flow, k], targets[u],
            ).start()

    def direct(flow, k):
        block = pl.ds(ROWS, ENTRY - ROWS)
        return remote(
            packed.at[flow, k, block], land.at[flow, k, block],
            send_a.at[flow, k], recv_a.at[flow, k], targets[1],
        )

    def group(flow, k, index):
        return land.at[flow, k, pl.ds(index * ENTRY, ENTRY)]

    def to_partner(flow, k):
        return remote(
            group(flow, k, 0), group(flow, k, 1), send_b.at[flow, k], recv_b.at[flow, k], partner
        )

    def to_sibling(flow, k):
        return remote(
            group(flow, k, 0), group(flow, k, 2), send_c.at[flow, k], recv_c.at[flow, k], sibling
        )

    def on_to_sibling(flow, k):
        return remote(
            group(flow, k, 1), group(flow, k, 3), send_d.at[flow, k], recv_d.at[flow, k], sibling
        )

    def enter(flow, k):
        direct(flow, k).wait_recv()
        to_partner(flow, k).start()
        to_sibling(flow, k).start()

    def pass_on(flow, k):
        to_partner(flow, k).wait_recv()
        on_to_sibling(flow, k).start()

    def unfold(flow, k):
        shape = (LEFT, ALL_ROWS)
        row = iota(shape, 0)
        taken = lax.div(row, 4) * ROWS + k * 4 + lax.rem(row, 4)
        return dot(one_hot(iota(shape, 1) == taken), land[flow, FOLD]).astype(BF16)

    def fold(k, rows):
        shape = (ALL_ROWS, LEFT)
        column = iota(shape, 1)
        taken = lax.div(column, 4) * ROWS + k * 4 + lax.rem(column, 4)
        return dot(one_hot(iota(shape, 0) == taken), rows)

    def digest(flow, k):
        to_sibling(flow, k).wait_recv()
        on_to_sibling(flow, k).wait_recv()
        out = pre_b if flow == SAVED else pre_f
        columns = slice(0, HID if flow == RETURNED else 2 * HID)

        def times(rows, c):
            return dot_t(rows, wout[c]) if flow == RETURNED else dot(rows, win[c])

        if k == 0:
            out[:ALL_ROWS, columns] = times(land[flow, k], k)
        elif k < CHUNKS:
            out[:ALL_ROWS, columns] += times(land[flow, k], k)
        else:
            rows = times(unfold(flow, 0), 0)
            for c in range(1, CHUNKS):
                rows = rows + times(unfold(flow, c), c)
            out[ALL_ROWS:, columns] = rows

    def make_hidden():
        @pl.loop(0, (ALL_ROWS + LEFT) // LEFT)
        def _(n):
            rows = pl.ds(pl.multiple_of(n * LEFT, LEFT), LEFT)
            gate_act = pre_f[rows, :HID]
            hidden[rows] = (gate_act * jax.nn.sigmoid(gate_act) * pre_f[rows, HID:]).astype(BF16)

    def make_pre_grad():
        @pl.loop(0, (ALL_ROWS + LEFT) // LEFT)
        def _(n):
            rows = pl.ds(pl.multiple_of(n * LEFT, LEFT), LEFT)
            hidden_grad = pre_f[rows, :HID]
            gate_act = pre_b[rows, :HID]
            up_act = pre_b[rows, HID:]
            sigmoid_gate = jax.nn.sigmoid(gate_act)
            up_grad = hidden_grad * (gate_act * sigmoid_gate)
            slope = sigmoid_gate * (1.0 + gate_act * (1.0 - sigmoid_gate))
            pre_grad[rows, :HID] = (hidden_grad * up_act * slope).astype(BF16)
            pre_grad[rows, HID:] = up_grad.astype(BF16)

    def product(way, rows, k):
        if way == FORWARD:
            return dot(hidden[rows], wout[k])
        return dot_t(pre_grad[rows], win[k])

    def swap(way, k):
        return remote(cross.at[k], sib.at[way, k], send_s.at[way, k], recv_s.at[way, k], sibling)

    def to_exit(way, k):
        return remote(pair_out.at[k], pair_in.at[way, k], send_p.at[way, k], recv_p.at[way, k], partner)

    def homeward(way, k):
        block = pl.ds(ROWS, ENTRY - ROWS)
        return remote(
            total.at[k, block], back.at[way, k, block], send_r.at[way, k], recv_r.at[way, k], sources[1]
        )

    def work(way, k):
        if way == BACKWARD:
            swap(FORWARD, k).wait_send()
        if k < CHUNKS:
            rows = product(way, slice(0, ALL_ROWS), k).astype(BF16)
            own[k] = rows[: 2 * ENTRY]
            cross[k] = rows[2 * ENTRY :]
        else:
            rows = jnp.zeros((ALL_ROWS, CHUNK), F32)
            for c in range(CHUNKS):
                rows = rows + fold(c, product(way, slice(ALL_ROWS, ALL_ROWS + LEFT), c).astype(BF16))
            rows = rows.astype(BF16)
            own[k] = rows[: 2 * ENTRY]
            cross[k] = rows[2 * ENTRY :]
        swap(way, k).start()

    def add_sibling(way, k):
        swap(way, k).wait_recv()
        if way == BACKWARD:
            to_exit(FORWARD, k).wait_send()
        rows = own[k, ENTRY:].astype(F32) + sib[way, k, ENTRY:].astype(F32)
        pair_out[k] = rows.astype(BF16)
        to_exit(way, k).start()

    def leave(way, k):
        to_exit(way, k).wait_recv()
        if way == BACKWARD:
            homeward(FORWARD, k).wait_send()
        rows = own[k, :ENTRY].astype(F32) + sib[way, k, :ENTRY].astype(F32)
        total[k] = (rows + pair_in[way, k].astype(F32)).astype(BF16)
        back[way, k, 0:ROWS] = total[k, 0:ROWS]
        for u in range(1, UNITS):
            block = pl.ds(u * ROWS, ROWS)
            remote(
                total.at[k, block], back.at[way, k, block],
                send_r.at[way, k], recv_r.at[way, k], sources[u],
            ).start()

    def written(way, k):
        columns = pl.ds(k * CHUNK, CHUNK)
        out = fwd_out if way == FORWARD else bwd_out
        return pltpu.make_async_copy(result.at[way, :, columns], out.at[:, columns], store.at[way, k])

    def place_rows(way, k):
        gate, base = ((fwd_gate, arrived), (bwd_gate, returned))[way]
        weight = jnp.broadcast_to(gate[...], (TOK, TOK)).T[:, :1]
        mixture = dot(placing[way, FOLD], back[way, k]) + dot(placing[way, k], back[way, FOLD])
        at_columns = slice(k * CHUNK, (k + 1) * CHUNK)
        rows = base[:, at_columns].astype(F32) + weight * mixture
        result[way, :, at_columns] = rows.astype(BF16)
        written(way, k).start()

    def finish(way, k):
        homeward(way, k).wait_recv()
        if k:
            place_rows(way, 0 if k == FOLD else k)

    make_masks(BACKWARD)
    loads[0].wait()
    pack(SAVED, 0)
    pl.semaphore_wait(barrier, len(peers))
    send(SAVED, 0)
    for k in range(1, CHUNKS + 1):
        pack(SAVED, k)
        if k < AHEAD:
            send(SAVED, k)
    make_masks(FORWARD)
    for copy in loads[1:]:
        copy.wait()

    steps = []

    def step(function, *arguments):
        steps.append((function, arguments))

    def take(flow, k):
        if flow != SAVED:
            if k < CHUNKS:
                move(FORWARD if flow == ARRIVED else BACKWARD, k).wait_recv()
            pack(flow, k)
        send(flow, k)

    def move_next(n):
        for way in (FORWARD, BACKWARD):
            if 0 <= n - MOVE_AT[way] < CHUNKS:
                move(way, n - MOVE_AT[way]).start()

    parts = CHUNKS + 1
    for n in range(3 * parts):
        flow, k = n // parts, n % parts
        step(enter, flow, k)
        step(move_next, n)
        if n + AHEAD < 3 * parts:
            step(take, (n + AHEAD) // parts, (n + AHEAD) % parts)
        if n:
            step(pass_on, (n - 1) // parts, (n - 1) % parts)
        if n >= 2:
            step(digest, (n - 2) // parts, (n - 2) % parts)
        if flow == RETURNED:
            if k == 1:
                step(make_hidden)
            if k >= 1:
                step(work, FORWARD, ORDER[k - 1])
            if k >= 2:
                step(add_sibling, FORWARD, ORDER[k - 2])
    step(pass_on, RETURNED, FOLD)
    step(work, FORWARD, ORDER[4])
    step(add_sibling, FORWARD, ORDER[3])
    step(leave, FORWARD, ORDER[0])
    step(add_sibling, FORWARD, ORDER[4])
    step(digest, RETURNED, 3)
    step(leave, FORWARD, ORDER[1])
    step(digest, RETURNED, FOLD)
    step(make_pre_grad)
    for j, k in enumerate(ORDER):
        if j >= 2:
            step(leave, FORWARD, k)
        step(work, BACKWARD, k)
        if j and j <= LAG:
            step(add_sibling, BACKWARD, ORDER[j - 1])
    for j, k in enumerate(ORDER):
        step(leave, BACKWARD, k)
        if j + LAG < parts:
            step(add_sibling, BACKWARD, ORDER[j + LAG])
        step(finish, FORWARD, k)
    for k in ORDER:
        step(finish, BACKWARD, k)
    for function, arguments in steps:
        function(*arguments)

    for way in (FORWARD, BACKWARD):
        for k in range(CHUNKS):
            move(way, k).wait_send()
    for flow in range(3):
        for k in range(CHUNKS + 1):
            direct(flow, k).wait_send()
            to_partner(flow, k).wait_send()
            to_sibling(flow, k).wait_send()
            on_to_sibling(flow, k).wait_send()
    for k in range(CHUNKS + 1):
        swap(BACKWARD, k).wait_send()
        to_exit(BACKWARD, k).wait_send()
        homeward(BACKWARD, k).wait_send()
    for way in (FORWARD, BACKWARD):
        for k in range(CHUNKS):
            written(way, k).wait()


def copy_kernel(fwd_in, bwd_in, fwd_out, bwd_out):
    fwd_out[0] = fwd_in[...]
    bwd_out[0] = bwd_in[...]


def keep(fwd_out, bwd_out):
    rows = TOK // 4
    return pl.pallas_call(
        copy_kernel,
        grid=(4,),
        out_shape=[jax.ShapeDtypeStruct((1, TOK, D), BF16)] * 2,
        in_specs=[pl.BlockSpec((rows, D), lambda n: (n, 0))] * 2,
        out_specs=[pl.BlockSpec((1, rows, D), lambda n: (0, n, 0))] * 2,
    )(fwd_out, bwd_out)


def local(fwd_in, fwd_route, fwd_gate, bwd_saved, bwd_route, bwd_gate, bwd_grad, w_in, w_out):
    any_place = pl.BlockSpec(memory_space=pl.ANY)
    vmem = pl.BlockSpec(memory_space=pltpu.VMEM)
    tokens = (TOK, D)
    parts = CHUNKS + 1
    dma = pltpu.SemaphoreType.DMA
    fwd_out, bwd_out = pl.pallas_call(
        kernel,
        out_shape=[jax.ShapeDtypeStruct(tokens, BF16)] * 2,
        in_specs=[any_place, vmem, vmem, any_place, vmem, vmem, any_place, any_place, any_place],
        out_specs=[any_place, any_place],
        scratch_shapes=[
            pltpu.VMEM(tokens, BF16),
            pltpu.VMEM(tokens, BF16),
            pltpu.VMEM(tokens, BF16),
            pltpu.VMEM((CHUNKS, CHUNK, 2 * HID), BF16),
            pltpu.VMEM((CHUNKS, HID, CHUNK), BF16),
            pltpu.VMEM((2, parts, TOK, TOK), BF16),
            pltpu.VMEM((2, parts, TOK, TOK), BF16),
            pltpu.VMEM((3, parts, ENTRY, CHUNK), BF16),
            pltpu.VMEM((3, parts, ALL_ROWS, CHUNK), BF16),
            pltpu.VMEM((ALL_ROWS + LEFT, 2 * HID), F32),
            pltpu.VMEM((ALL_ROWS + LEFT, 2 * HID), F32),
            pltpu.VMEM((ALL_ROWS + LEFT, HID), BF16),
            pltpu.VMEM((ALL_ROWS + LEFT, 2 * HID), BF16),
            pltpu.VMEM((parts, 2 * ENTRY, CHUNK), BF16),
            pltpu.VMEM((parts, 2 * ENTRY, CHUNK), BF16),
            pltpu.VMEM((2, parts, 2 * ENTRY, CHUNK), BF16),
            pltpu.VMEM((parts, ENTRY, CHUNK), BF16),
            pltpu.VMEM((2, parts, ENTRY, CHUNK), BF16),
            pltpu.VMEM((parts, ENTRY, CHUNK), BF16),
            pltpu.VMEM((2, parts, ENTRY, CHUNK), BF16),
            pltpu.VMEM((2, TOK, D), BF16),
        ]
        + [dma((3, parts))] * 8
        + [dma((2, parts))] * 6
        + [dma((2, CHUNKS))] * 2
        + [dma((9,)), dma((2, CHUNKS))],
        compiler_params=pltpu.CompilerParams(
            collective_id=0, has_side_effects=True, vmem_limit_bytes=60 * 2**20
        ),
        cost_estimate=pl.CostEstimate(
            flops=14 * 10**9, bytes_accessed=14 * 10**6, transcendentals=500_000
        ),
    )(
        fwd_in[0], fwd_route.reshape(1, TOK), fwd_gate.reshape(1, TOK),
        bwd_saved[0], bwd_route.reshape(1, TOK), bwd_gate.reshape(1, TOK), bwd_grad[0],
        w_in[0, 0], w_out[0, 0],
    )
    return keep(fwd_out, bwd_out)


def solution(mesh):
    rows = P("pipe", "expert", None)
    pieces = P("pipe", "expert", None, None)
    return jax.shard_map(
        local,
        mesh=mesh,
        in_specs=(rows,) * 7 + (pieces,) * 2,
        out_specs=(rows, rows),
        check_vma=False,
    )
```

```python
import jax
import jax.numpy as jnp
from jax import lax
from jax.experimental import pallas as pl
from jax.experimental.pallas import tpu as pltpu
from jax.sharding import PartitionSpec as P

MESH = pl.DeviceIdType.MESH
SCHEDULE = ((), ((0, 0),), ((0, 1),), ((0, 2),), ((0, 3), (1, 0), (1, 1)))
TOK = 128
D = 3584
HID = 384
ROWS = 16
CHUNK = 896
CHUNKS = 4
FOLD = 4
UNITS = 8
PIECES = 4
ENTRY = UNITS * ROWS
ALL_ROWS = 4 * ENTRY
LEFT = 128
OFFSETS = (0, -1, 2, -3)
ORDER = (0, 4, 1, 2, 3)
MOVE_AT = (0, 3)
LAG = 4
AHEAD = 4
SAVED, ARRIVED, RETURNED = 0, 1, 2
FORWARD, BACKWARD = 0, 1
F32 = jnp.float32
BF16 = jnp.bfloat16


def dot(a, b):
    return lax.dot_general(a, b, (((1,), (0,)), ((), ())), preferred_element_type=F32)


def dot_t(a, b):
    return lax.dot_general(a, b, (((1,), (1,)), ((), ())), preferred_element_type=F32)


def iota(shape, dim):
    return lax.broadcasted_iota(jnp.int32, shape, dim)


def one_hot(mask):
    return jnp.where(mask, 1.0, 0.0).astype(BF16)


def kernel(
    fwd_in, fwd_route, fwd_gate, bwd_saved, bwd_route, bwd_gate, bwd_grad, w_in, w_out,
    fwd_out, bwd_out,
    saved, arrived, returned, win, wout, packing, placing, packed, land, pre_f, pre_b, hidden, pre_grad,
    own, cross, sib, pair_out, pair_in, total, back, result,
    send_a, recv_a, send_b, recv_b, send_c, recv_c, send_d, recv_d,
    send_s, recv_s, send_p, recv_p, send_r, recv_r, send_m, recv_m, load, store,
):
    pipe = lax.axis_index("pipe")
    place = lax.axis_index("expert")
    y = lax.div(place, 16)
    z = lax.rem(lax.div(place, 2), 8)
    core = lax.rem(place, 2)
    side = 1 - 2 * lax.rem(z, 2)

    def device(pipe_at, y_at, z_at, core_at):
        return (pipe_at, y_at * 16 + z_at * 2 + core_at)

    def at(y_step, z_step):
        return lax.rem(y + y_step, 2), lax.rem(z + z_step + 8, 8)

    targets, experts, sources = [], [], []
    for i in range(4):
        for y_step in range(2):
            y_to, z_to = at(y_step, OFFSETS[i] * side)
            targets.append(device(pipe, y_to, z_to, core))
            experts.append(y_to * 4 + lax.div(z_to, 2))
            y_from, z_from = at(y_step, -i * side)
            sources.append(device(pipe, y_from, z_from, core))
    sibling = device(pipe, y, z, 1 - core)
    partner = device(pipe, y, lax.rem(z + side + 8, 8), core)
    after = (lax.rem(pipe + 1, 8), place)
    before = (lax.rem(pipe + 7, 8), place)

    loads = [pltpu.make_async_copy(bwd_saved, saved, load.at[0])]
    for k in range(CHUNKS):
        columns = pl.ds(k * CHUNK, CHUNK)
        loads.append(pltpu.make_async_copy(w_in.at[columns], win.at[k], load.at[1 + k]))
        loads.append(pltpu.make_async_copy(w_out.at[:, columns], wout.at[k], load.at[5 + k]))
    for copy in loads:
        copy.start()

    barrier = pltpu.get_barrier_semaphore()
    peers = targets[1:] + sources[4:6] + [sibling, partner, after, before]
    for peer in peers:
        pl.semaphore_signal(barrier, inc=1, device_id=peer, device_id_type=MESH)

    def remote(src, dst, send, recv, to):
        return pltpu.make_async_remote_copy(
            src_ref=src, dst_ref=dst, send_sem=send, recv_sem=recv, device_id=to, device_id_type=MESH
        )

    def move(way, k):
        columns = pl.ds(k * CHUNK, CHUNK)
        src, dst, to = ((fwd_in, arrived, after), (bwd_grad, returned, before))[way]
        return remote(src.at[:, columns], dst.at[:, columns], send_m.at[way, k], recv_m.at[way, k], to)

    def unit_experts(shape, dim):
        unit = lax.div(iota(shape, dim), ROWS)
        named = jnp.zeros(shape, jnp.int32)
        for u in range(UNITS):
            named = jnp.where(unit == u, experts[u], named)
        return named

    def make_masks(way):
        square = (TOK, TOK)
        route = (fwd_route, bwd_route)[way]
        by_lane = jnp.broadcast_to(route[...], square).astype(F32)
        by_row = by_lane.T
        same = by_row == by_lane
        lane, sublane = iota(square, 1), iota(square, 0)

        slot = jnp.sum(jnp.where(same & (sublane < lane), 1.0, 0.0), axis=0, keepdims=True)
        named = unit_experts(square, 0).astype(F32) == by_lane
        row = lax.rem(sublane, ROWS)
        packing[way, FOLD] = one_hot(named & (row.astype(F32) == slot))
        late = named & ((ROWS + lax.rem(row, 4)).astype(F32) == slot)
        for k in range(CHUNKS):
            packing[way, k] = one_hot(late & (lax.div(row, 4) == k))

        slot = jnp.sum(jnp.where(same & (lane < sublane), 1.0, 0.0), axis=1, keepdims=True)
        named = unit_experts(square, 1).astype(F32) == by_row
        column = lax.rem(lane, ROWS)
        placing[way, FOLD] = one_hot(named & (column.astype(F32) == slot))
        late = named & ((ROWS + lax.rem(column, 4)).astype(F32) == slot)
        for k in range(CHUNKS):
            placing[way, k] = one_hot(late & (lax.div(column, 4) == k))

    def pack(flow, k):
        values = (saved, arrived, returned)[flow]
        way = FORWARD if flow == ARRIVED else BACKWARD
        if k < CHUNKS:
            rows = dot(packing[way, FOLD], values[:, k * CHUNK : (k + 1) * CHUNK])
        else:
            rows = jnp.zeros((ENTRY, CHUNK), F32)
            for c in range(CHUNKS):
                rows = rows + dot(packing[way, c], values[:, c * CHUNK : (c + 1) * CHUNK])
        packed[flow, k] = rows.astype(BF16)
        land[flow, k, 0:ROWS] = packed[flow, k, 0:ROWS]

    def send(flow, k):
        for u in range(1, UNITS):
            block = pl.ds(u * ROWS, ROWS)
            remote(
                packed.at[flow, k, block], land.at[flow, k, block],
                send_a.at[flow, k], recv_a.at[flow, k], targets[u],
            ).start()

    def direct(flow, k):
        block = pl.ds(ROWS, ENTRY - ROWS)
        return remote(
            packed.at[flow, k, block], land.at[flow, k, block],
            send_a.at[flow, k], recv_a.at[flow, k], targets[1],
        )

    def group(flow, k, index):
        return land.at[flow, k, pl.ds(index * ENTRY, ENTRY)]

    def to_partner(flow, k):
        return remote(
            group(flow, k, 0), group(flow, k, 1), send_b.at[flow, k], recv_b.at[flow, k], partner
        )

    def to_sibling(flow, k):
        return remote(
            group(flow, k, 0), group(flow, k, 2), send_c.at[flow, k], recv_c.at[flow, k], sibling
        )

    def on_to_sibling(flow, k):
        return remote(
            group(flow, k, 1), group(flow, k, 3), send_d.at[flow, k], recv_d.at[flow, k], sibling
        )

    def enter(flow, k):
        direct(flow, k).wait_recv()
        to_partner(flow, k).start()
        to_sibling(flow, k).start()

    def pass_on(flow, k):
        to_partner(flow, k).wait_recv()
        on_to_sibling(flow, k).start()

    def unfold(flow, k):
        shape = (LEFT, ALL_ROWS)
        row = iota(shape, 0)
        taken = lax.div(row, 4) * ROWS + k * 4 + lax.rem(row, 4)
        return dot(one_hot(iota(shape, 1) == taken), land[flow, FOLD]).astype(BF16)

    def fold(k, rows):
        shape = (ALL_ROWS, LEFT)
        column = iota(shape, 1)
        taken = lax.div(column, 4) * ROWS + k * 4 + lax.rem(column, 4)
        return dot(one_hot(iota(shape, 0) == taken), rows)

    def digest(flow, k):
        to_sibling(flow, k).wait_recv()
        on_to_sibling(flow, k).wait_recv()
        out = pre_b if flow == SAVED else pre_f
        columns = slice(0, HID if flow == RETURNED else 2 * HID)

        def times(rows, c):
            return dot_t(rows, wout[c]) if flow == RETURNED else dot(rows, win[c])

        if k == 0:
            out[:ALL_ROWS, columns] = times(land[flow, k], k)
        elif k < CHUNKS:
            out[:ALL_ROWS, columns] += times(land[flow, k], k)
        else:
            rows = times(unfold(flow, 0), 0)
            for c in range(1, CHUNKS):
                rows = rows + times(unfold(flow, c), c)
            out[ALL_ROWS:, columns] = rows

    def make_hidden():
        @pl.loop(0, (ALL_ROWS + LEFT) // LEFT)
        def _(n):
            rows = pl.ds(pl.multiple_of(n * LEFT, LEFT), LEFT)
            gate_act = pre_f[rows, :HID]
            hidden[rows] = (gate_act * jax.nn.sigmoid(gate_act) * pre_f[rows, HID:]).astype(BF16)

    def make_pre_grad():
        @pl.loop(0, (ALL_ROWS + LEFT) // LEFT)
        def _(n):
            rows = pl.ds(pl.multiple_of(n * LEFT, LEFT), LEFT)
            hidden_grad = pre_f[rows, :HID]
            gate_act = pre_b[rows, :HID]
            up_act = pre_b[rows, HID:]
            sigmoid_gate = jax.nn.sigmoid(gate_act)
            up_grad = hidden_grad * (gate_act * sigmoid_gate)
            slope = sigmoid_gate * (1.0 + gate_act * (1.0 - sigmoid_gate))
            pre_grad[rows, :HID] = (hidden_grad * up_act * slope).astype(BF16)
            pre_grad[rows, HID:] = up_grad.astype(BF16)

    def product(way, rows, k):
        if way == FORWARD:
            return dot(hidden[rows], wout[k])
        return dot_t(pre_grad[rows], win[k])

    def swap(way, k):
        return remote(cross.at[k], sib.at[way, k], send_s.at[way, k], recv_s.at[way, k], sibling)

    def to_exit(way, k):
        return remote(pair_out.at[k], pair_in.at[way, k], send_p.at[way, k], recv_p.at[way, k], partner)

    def homeward(way, k):
        block = pl.ds(ROWS, ENTRY - ROWS)
        return remote(
            total.at[k, block], back.at[way, k, block], send_r.at[way, k], recv_r.at[way, k], sources[1]
        )

    def work(way, k):
        if way == BACKWARD:
            swap(FORWARD, k).wait_send()
        if k < CHUNKS:
            rows = product(way, slice(0, ALL_ROWS), k).astype(BF16)
            own[k] = rows[: 2 * ENTRY]
            cross[k] = rows[2 * ENTRY :]
        else:
            rows = jnp.zeros((ALL_ROWS, CHUNK), F32)
            for c in range(CHUNKS):
                rows = rows + fold(c, product(way, slice(ALL_ROWS, ALL_ROWS + LEFT), c).astype(BF16))
            rows = rows.astype(BF16)
            own[k] = rows[: 2 * ENTRY]
            cross[k] = rows[2 * ENTRY :]
        swap(way, k).start()

    def add_sibling(way, k):
        swap(way, k).wait_recv()
        if way == BACKWARD:
            to_exit(FORWARD, k).wait_send()
        rows = own[k, ENTRY:].astype(F32) + sib[way, k, ENTRY:].astype(F32)
        pair_out[k] = rows.astype(BF16)
        to_exit(way, k).start()

    def leave(way, k):
        to_exit(way, k).wait_recv()
        if way == BACKWARD:
            homeward(FORWARD, k).wait_send()
        rows = own[k, :ENTRY].astype(F32) + sib[way, k, :ENTRY].astype(F32)
        total[k] = (rows + pair_in[way, k].astype(F32)).astype(BF16)
        back[way, k, 0:ROWS] = total[k, 0:ROWS]
        for u in range(1, UNITS):
            block = pl.ds(u * ROWS, ROWS)
            remote(
                total.at[k, block], back.at[way, k, block],
                send_r.at[way, k], recv_r.at[way, k], sources[u],
            ).start()

    def written(way, k):
        columns = pl.ds(k * CHUNK, CHUNK)
        out = fwd_out if way == FORWARD else bwd_out
        return pltpu.make_async_copy(result.at[way, :, columns], out.at[:, columns], store.at[way, k])

    def place_rows(way, k):
        gate, base = ((fwd_gate, arrived), (bwd_gate, returned))[way]
        weight = jnp.broadcast_to(gate[...], (TOK, TOK)).T[:, :1]
        mixture = dot(placing[way, FOLD], back[way, k]) + dot(placing[way, k], back[way, FOLD])
        at_columns = slice(k * CHUNK, (k + 1) * CHUNK)
        rows = base[:, at_columns].astype(F32) + weight * mixture
        result[way, :, at_columns] = rows.astype(BF16)
        written(way, k).start()

    def finish(way, k):
        homeward(way, k).wait_recv()
        if k:
            place_rows(way, 0 if k == FOLD else k)

    make_masks(BACKWARD)
    loads[0].wait()
    pack(SAVED, 0)
    pl.semaphore_wait(barrier, len(peers))
    send(SAVED, 0)
    for k in range(1, CHUNKS + 1):
        pack(SAVED, k)
        if k < AHEAD:
            send(SAVED, k)
    make_masks(FORWARD)
    for copy in loads[1:]:
        copy.wait()

    steps = []

    def step(function, *arguments):
        steps.append((function, arguments))

    def take(flow, k):
        if flow != SAVED:
            if k < CHUNKS:
                move(FORWARD if flow == ARRIVED else BACKWARD, k).wait_recv()
            pack(flow, k)
        send(flow, k)

    def move_next(n):
        for way in (FORWARD, BACKWARD):
            if 0 <= n - MOVE_AT[way] < CHUNKS:
                move(way, n - MOVE_AT[way]).start()

    parts = CHUNKS + 1
    for n in range(3 * parts):
        flow, k = n // parts, n % parts
        step(enter, flow, k)
        step(move_next, n)
        if n + AHEAD < 3 * parts:
            step(take, (n + AHEAD) // parts, (n + AHEAD) % parts)
        if n:
            step(pass_on, (n - 1) // parts, (n - 1) % parts)
        if n >= 2:
            step(digest, (n - 2) // parts, (n - 2) % parts)
        if flow == RETURNED:
            if k == 1:
                step(make_hidden)
            for function, number in SCHEDULE[k]:
                step((work, add_sibling, leave)[function], FORWARD, ORDER[number])
    step(pass_on, RETURNED, FOLD)
    step(work, FORWARD, ORDER[4])
    for number in (2, 3, 4):
        step(add_sibling, FORWARD, ORDER[number])
    step(digest, RETURNED, 3)
    step(leave, FORWARD, ORDER[0])
    step(digest, RETURNED, FOLD)
    step(leave, FORWARD, ORDER[1])
    step(make_pre_grad)
    for j, k in enumerate(ORDER):
        if j >= 2:
            step(leave, FORWARD, k)
        step(work, BACKWARD, k)
        if j and j <= LAG:
            step(add_sibling, BACKWARD, ORDER[j - 1])
    for j, k in enumerate(ORDER):
        step(leave, BACKWARD, k)
        if j + LAG < parts:
            step(add_sibling, BACKWARD, ORDER[j + LAG])
        step(finish, FORWARD, k)
    for k in ORDER:
        step(finish, BACKWARD, k)
    for function, arguments in steps:
        function(*arguments)

    for way in (FORWARD, BACKWARD):
        for k in range(CHUNKS):
            move(way, k).wait_send()
    for flow in range(3):
        for k in range(CHUNKS + 1):
            direct(flow, k).wait_send()
            to_partner(flow, k).wait_send()
            to_sibling(flow, k).wait_send()
            on_to_sibling(flow, k).wait_send()
    for k in range(CHUNKS + 1):
        swap(BACKWARD, k).wait_send()
        to_exit(BACKWARD, k).wait_send()
        homeward(BACKWARD, k).wait_send()
    for way in (FORWARD, BACKWARD):
        for k in range(CHUNKS):
            written(way, k).wait()


def copy_kernel(fwd_in, bwd_in, fwd_out, bwd_out, held, read, wrote):
    reads, writes = [], []
    for way, (src, dst) in enumerate(((fwd_in, fwd_out), (bwd_in, bwd_out))):
        for n in range(PIECES):
            rows = pl.ds(n * (TOK // PIECES), TOK // PIECES)
            reads.append(pltpu.make_async_copy(src.at[rows], held.at[way, rows], read.at[way, n]))
            writes.append(pltpu.make_async_copy(held.at[way, rows], dst.at[0, rows], wrote.at[way, n]))
    for copy in reads:
        copy.start()
    for arrived, leaving in zip(reads, writes):
        arrived.wait()
        leaving.start()
    for copy in writes:
        copy.wait()


def keep(fwd_out, bwd_out):
    any_place = pl.BlockSpec(memory_space=pl.ANY)
    dma = pltpu.SemaphoreType.DMA
    return pl.pallas_call(
        copy_kernel,
        out_shape=[jax.ShapeDtypeStruct((1, TOK, D), BF16)] * 2,
        in_specs=[any_place] * 2,
        out_specs=[any_place] * 2,
        scratch_shapes=[pltpu.VMEM((2, TOK, D), BF16), dma((2, PIECES)), dma((2, PIECES))],
    )(fwd_out, bwd_out)


def local(fwd_in, fwd_route, fwd_gate, bwd_saved, bwd_route, bwd_gate, bwd_grad, w_in, w_out):
    any_place = pl.BlockSpec(memory_space=pl.ANY)
    vmem = pl.BlockSpec(memory_space=pltpu.VMEM)
    tokens = (TOK, D)
    parts = CHUNKS + 1
    dma = pltpu.SemaphoreType.DMA
    fwd_out, bwd_out = pl.pallas_call(
        kernel,
        out_shape=[jax.ShapeDtypeStruct(tokens, BF16)] * 2,
        in_specs=[any_place, vmem, vmem, any_place, vmem, vmem, any_place, any_place, any_place],
        out_specs=[any_place, any_place],
        scratch_shapes=[
            pltpu.VMEM(tokens, BF16),
            pltpu.VMEM(tokens, BF16),
            pltpu.VMEM(tokens, BF16),
            pltpu.VMEM((CHUNKS, CHUNK, 2 * HID), BF16),
            pltpu.VMEM((CHUNKS, HID, CHUNK), BF16),
            pltpu.VMEM((2, parts, TOK, TOK), BF16),
            pltpu.VMEM((2, parts, TOK, TOK), BF16),
            pltpu.VMEM((3, parts, ENTRY, CHUNK), BF16),
            pltpu.VMEM((3, parts, ALL_ROWS, CHUNK), BF16),
            pltpu.VMEM((ALL_ROWS + LEFT, 2 * HID), F32),
            pltpu.VMEM((ALL_ROWS + LEFT, 2 * HID), F32),
            pltpu.VMEM((ALL_ROWS + LEFT, HID), BF16),
            pltpu.VMEM((ALL_ROWS + LEFT, 2 * HID), BF16),
            pltpu.VMEM((parts, 2 * ENTRY, CHUNK), BF16),
            pltpu.VMEM((parts, 2 * ENTRY, CHUNK), BF16),
            pltpu.VMEM((2, parts, 2 * ENTRY, CHUNK), BF16),
            pltpu.VMEM((parts, ENTRY, CHUNK), BF16),
            pltpu.VMEM((2, parts, ENTRY, CHUNK), BF16),
            pltpu.VMEM((parts, ENTRY, CHUNK), BF16),
            pltpu.VMEM((2, parts, ENTRY, CHUNK), BF16),
            pltpu.VMEM((2, TOK, D), BF16),
        ]
        + [dma((3, parts))] * 8
        + [dma((2, parts))] * 6
        + [dma((2, CHUNKS))] * 2
        + [dma((9,)), dma((2, CHUNKS))],
        compiler_params=pltpu.CompilerParams(
            collective_id=0, has_side_effects=True, vmem_limit_bytes=60 * 2**20
        ),
        cost_estimate=pl.CostEstimate(
            flops=14 * 10**9, bytes_accessed=14 * 10**6, transcendentals=500_000
        ),
    )(
        fwd_in[0], fwd_route.reshape(1, TOK), fwd_gate.reshape(1, TOK),
        bwd_saved[0], bwd_route.reshape(1, TOK), bwd_gate.reshape(1, TOK), bwd_grad[0],
        w_in[0, 0], w_out[0, 0],
    )
    return keep(fwd_out, bwd_out)


def solution(mesh):
    rows = P("pipe", "expert", None)
    pieces = P("pipe", "expert", None, None)
    return jax.shard_map(
        local,
        mesh=mesh,
        in_specs=(rows,) * 7 + (pieces,) * 2,
        out_specs=(rows, rows),
        check_vma=False,
    )
```
